32 devices in a mesh: row: 4 (over z), col: 4 (over x, core), dp: 2 (over y).
Axes of the slice: x: 2, y: 2, z: 4, core: 2. Of those that a mesh axis runs over, the one named last changes fastest.
Arguments:
- activations: bfloat16 [2, 1536, 4096], P('dp', 'row', 'col'), may hold values from -6 to 6
- cotangent: bfloat16 [2, 1536, 4096], P('dp', 'row', 'col'), may hold values from -6 to 6
- gate_weight: bfloat16 [4096, 8192], P('col', 'row'), may hold values from -0.09375 to 0.09375
- up_weight: bfloat16 [4096, 8192], P('col', 'row'), may hold values from -0.09375 to 0.09375
- down_weight: bfloat16 [8192, 4096], P('row', 'col'), may hold values from -0.0625 to 0.0625
- probes: bfloat16 [2, 4096, 8192], P(None, 'col', 'row'), may hold values from -1 to 1, as said below
Outputs:
- outputs: bfloat16 [2, 1536, 4096], P('dp', 'row', 'col')
- diag_estimate: float32 [4096, 8192], P('col', ('row', 'dp'))
The draws below stay inside these ranges and needn't reach their ends.
Inputs may be any that keep to these rules, and one draw needn't show every extreme that they name: `probes`: every entry is +1 or -1.
All inputs are finite; a program needn't handle non-finite values.
Results may differ from the reference program's by a relative error of at most 0.005.
Values may be sent and summed in bfloat16 or wider, within the bound.
A program may use at most 256 MiB of HBM per device.

```python
import jax
import jax.numpy as jnp

D = 4096
F = 8192
TOK = 1536
NPROBE = 2
GROUPS = 2


def draw_probes(key, part):
    flips = jax.random.bernoulli(key, 0.5, (NPROBE, D, F))
    return jnp.where(flips, 1.0, -1.0).astype(jnp.float32).astype(jnp.bfloat16)


def levels(rng, dims, shards, low, largest):
    level, own = 1.0, jax.random.fold_in(rng, 6)
    for dim, blocks in shards:
        draws = jnp.exp(jax.random.uniform(jax.random.fold_in(own, dim), (blocks,), jnp.float32, low / len(shards), largest / len(shards)))
        level = level * jnp.repeat(draws, dims[dim] // blocks).reshape([-1 if axis == dim else 1 for axis in range(len(dims))])
    return level


def normal_values(key, shape, deviation, most, cuts=(), held_as=jnp.bfloat16):
    array = jax.random.normal(key, shape, jnp.float32) * deviation
    if len(cuts) > 0:
        array = levels(key, shape, cuts, -0.22, 0.18) * array
    return jnp.clip(array, min=-most, max=most).astype(held_as)


def setup_inputs(seed: int = 0) -> dict:
    splits = jax.random.split(jax.random.key(seed), 7)
    return {
        "activations": normal_values(splits[0], (GROUPS, TOK, D), 1.0, 6.0, ((0, 2), (1, 4), (2, 4))),
        "cotangent": normal_values(splits[1], (GROUPS, TOK, D), 1.0, 6.0, ((0, 2), (1, 4), (2, 4))),
        "gate_weight": normal_values(splits[2], (D, F), D ** -0.5, 0.09375, ((0, 4), (1, 4))),
        "up_weight": normal_values(splits[3], (D, F), D ** -0.5, 0.09375, ((0, 4), (1, 4))),
        "down_weight": normal_values(splits[4], (F, D), F ** -0.5, 0.0625, ((0, 4), (1, 4))),
        "probes": draw_probes(jax.random.fold_in(splits[6], 71), 0),
    }


def curvature_terms(features, cot_rows, gate_weight, up_weight, down_weight):
    gate_sum = jnp.dot(features, gate_weight, preferred_element_type=jnp.float32)
    up_sum = jnp.dot(features, up_weight, preferred_element_type=jnp.float32)
    error_sum = jnp.dot(cot_rows, down_weight.T, preferred_element_type=jnp.float32)
    sigma = jax.nn.sigmoid(gate_sum)
    hidden = (gate_sum * sigma * up_sum).astype(jnp.bfloat16)
    bending = error_sum * up_sum * sigma * (1.0 - sigma) * (2.0 + gate_sum * (1.0 - 2.0 * sigma))
    return hidden, bending


def reference(activations, cotangent, gate_weight, up_weight, down_weight, probes):
    results = []
    total = jnp.zeros((D, F), jnp.float32)
    for group in range(GROUPS):
        features = activations[group]
        hidden, bending = curvature_terms(features, cotangent[group], gate_weight, up_weight, down_weight)
        results.append(jnp.dot(hidden, down_weight, preferred_element_type=jnp.float32).astype(jnp.bfloat16))
        for probe in range(NPROBE):
            tangent = jnp.dot(features, probes[probe], preferred_element_type=jnp.float32)
            weighted = (bending * tangent).astype(jnp.bfloat16)
            curvature = jnp.dot(features.T, weighted, preferred_element_type=jnp.float32)
            total = total + probes[probe].astype(jnp.float32) * curvature
    diag_estimate = total * (1.0 / (NPROBE * GROUPS * TOK))
    return jnp.stack(results), diag_estimate
```

```python
import jax
import jax.numpy as jnp
from jax import lax
from jax.sharding import PartitionSpec as P

NEAR = jnp.bfloat16
FAR = jnp.bfloat16


def swap(value, axis, bit):
    pairs = [(i, i ^ bit) for i in range(lax.axis_size(axis))]
    return lax.ppermute(value, axis, pairs)


def local(activations, cotangent, gate_weight, up_weight, down_weight, probes):
    f32, bf16 = jnp.float32, jnp.bfloat16
    assert lax.axis_size("col") == 4 and lax.axis_size("dp") == 2
    col, row, group = lax.axis_index("col"), lax.axis_index("row"), lax.axis_index("dp")
    near, far = col % 2, col // 2
    mine = activations.shape[1]
    tokens = mine * lax.axis_size("row")
    width = gate_weight.shape[1]
    chunk, half, quarter = width // 2, width // 4, width // 8

    def turned(array, start):
        return lax.dynamic_slice_in_dim(jnp.concatenate([array, array], axis=0), start, tokens, axis=0)

    everyone = lax.all_gather(activations, "row", axis=1, tiled=True)[0]
    features = turned(everyone, row * mine)
    later_cot, _ = lax.optimization_barrier((cotangent, everyone))
    cot = turned(lax.all_gather(later_cot, "row", axis=1, tiled=True)[0], row * mine)
    acts_parts = [activations[0], features[mine:]]
    cot_parts = [cotangent[0], cot[mine:]]
    bases = [(1 - group) * chunk, group * chunk]
    sent = []

    def crossing(value):
        if sent:
            value, _ = lax.optimization_barrier((value, sent[-1]))
        sent.append(value)
        return swap(value, "col", 2)

    def own(base):
        return base + near * half

    def others(base):
        return base + (1 - near) * half

    def columns(array, start):
        return lax.dynamic_slice_in_dim(array, start, half, axis=1)

    def rows(array, start):
        return lax.dynamic_slice_in_dim(array, start, half, axis=0)

    def pick(value, which):
        return lax.dynamic_slice_in_dim(value, which * quarter, quarter, axis=1)

    def forward(weight):
        def product(part, start):
            return jnp.dot(acts_parts[part], columns(weight, start), preferred_element_type=f32)
        return product

    def backward(part, start):
        return lax.dot_general(
            cot_parts[part], rows(down_weight, start), (((1,), (1,)), ((), ())), preferred_element_type=f32
        )

    kinds = {"gate": forward(gate_weight), "up": forward(up_weight), "error": backward}
    for index in range(probes.shape[0]):
        kinds["tangent", index] = forward(probes[index])
    tangent_names = [("tangent", index) for index in range(probes.shape[0])]
    summed = {}

    def reduce(name, which, part):
        product, base = kinds[name], bases[which]
        came = swap(product(part, others(base)).astype(NEAR), "col", 1)
        both = product(part, own(base)) + came.astype(f32)
        crossed = crossing(pick(both, 1 - far).astype(FAR))
        summed[name, which, part] = (pick(both, far), crossed)

    def total(name, which):
        parts = [summed[name, which, part] for part in range(2)]
        return jnp.concatenate([kept + crossed.astype(f32) for kept, crossed in parts], axis=0)

    def gathered(value):
        crossed = crossing(value)
        ahead = jnp.concatenate([value, crossed], axis=1)
        behind = jnp.concatenate([crossed, value], axis=1)
        both = jnp.where(far == 0, ahead, behind)
        return both, swap(both, "col", 1)

    for which in range(2):
        for name in ("gate", "up"):
            reduce(name, which, 0)
    for which in range(2):
        for name in tangent_names + ["error"]:
            reduce(name, which, 0)
    for which in range(2):
        for name in ("gate", "up"):
            reduce(name, which, 1)
    for name in tangent_names:
        reduce(name, 0, 1)
    gates = [total("gate", which) for which in range(2)]
    ups = [total("up", which) for which in range(2)]
    sigmas = [jax.nn.sigmoid(gate) for gate in gates]
    hidden = []
    for gate, sigma, up in zip(gates, sigmas, ups):
        hidden.extend(gathered((gate * sigma * up).astype(bf16)))
    order = [place(base) for base in bases for place in (own, others)]
    down = jnp.concatenate([rows(down_weight, start) for start in order], axis=0)
    partial = jnp.dot(jnp.concatenate(hidden, axis=1), down, preferred_element_type=f32)
    partial = turned(partial, tokens - row * mine)
    outputs = lax.psum_scatter(partial, "row", scatter_dimension=0, tiled=True).astype(bf16)[None]

    scale = 1.0 / (probes.shape[0] * lax.axis_size("dp") * tokens)

    def weighted(which):
        gate, sigma, up = gates[which], sigmas[which], ups[which]
        bending = total("error", which) * up * sigma * (1.0 - sigma) * (2.0 + gate * (1.0 - 2.0 * sigma))
        return [gathered((bending * total(name, which)).astype(bf16)) for name in tangent_names]

    def estimate(pieces, which, side):
        start = (own, others)[side](bases[which])
        result = 0.0
        for probe, piece in zip(probes, pieces):
            curvature = lax.dot_general(features, piece[side], (((0,), (0,)), ((), ())), preferred_element_type=f32)
            result = result + columns(probe, start).astype(f32) * curvature
        return result * scale

    reduce("error", 0, 1)
    reduce(tangent_names[0], 1, 1)
    pieces = weighted(0)
    came = [swap(estimate(pieces, 0, side), "dp", 1) for side in range(2)]
    for name in tangent_names[1:] + ["error"]:
        reduce(name, 1, 1)
    pieces = weighted(1)
    first, second = [estimate(pieces, 1, side) + came[side] for side in range(2)]
    diagonal = jnp.where(
        near == 0,
        jnp.concatenate([first, second], axis=1),
        jnp.concatenate([second, first], axis=1),
    )
    return outputs, diagonal


def solution(mesh):
    in_specs = (
        P("dp", "row", "col"),
        P("dp", "row", "col"),
        P("col", "row"),
        P("col", "row"),
        P("row", "col"),
        P(None, "col", "row"),
    )
    out_specs = (P("dp", "row", "col"), P("col", ("row", "dp")))
    return jax.shard_map(local, mesh=mesh, in_specs=in_specs, out_specs=out_specs, check_vma=False)
```

```python
import jax
import jax.numpy as jnp
from jax import lax
from jax.sharding import PartitionSpec as P

NEAR = jnp.bfloat16
FAR = jnp.bfloat16


def swap(value, axis, bit):
    pairs = [(i, i ^ bit) for i in range(lax.axis_size(axis))]
    return lax.ppermute(value, axis, pairs)


def local(activations, cotangent, gate_weight, up_weight, down_weight, probes):
    f32, bf16 = jnp.float32, jnp.bfloat16
    assert lax.axis_size("col") == 4 and lax.axis_size("dp") == 2
    col, row, group = lax.axis_index("col"), lax.axis_index("row"), lax.axis_index("dp")
    near, far = col % 2, col // 2
    mine = activations.shape[1]
    tokens = mine * lax.axis_size("row")
    width = gate_weight.shape[1]
    chunk, half, quarter = width // 2, width // 4, width // 8

    def turned(array, start):
        return lax.dynamic_slice_in_dim(jnp.concatenate([array, array], axis=0), start, tokens, axis=0)

    everyone = lax.all_gather(activations, "row", axis=1, tiled=True)[0]
    features = turned(everyone, row * mine)
    later_cot, _ = lax.optimization_barrier((cotangent, everyone))
    cot = turned(lax.all_gather(later_cot, "row", axis=1, tiled=True)[0], row * mine)
    acts_parts = [activations[0], features[mine:]]
    cot_parts = [cotangent[0], cot[mine:]]
    bases = [(1 - group) * chunk, group * chunk]
    sent = []

    def crossing(value):
        if sent:
            value, _ = lax.optimization_barrier((value, sent[-1]))
        sent.append(value)
        return swap(value, "col", 2)

    def own(base):
        return base + near * half

    def others(base):
        return base + (1 - near) * half

    def columns(array, start):
        return lax.dynamic_slice_in_dim(array, start, half, axis=1)

    def rows(array, start):
        return lax.dynamic_slice_in_dim(array, start, half, axis=0)

    def pick(value, which):
        return lax.dynamic_slice_in_dim(value, which * quarter, quarter, axis=1)

    def forward(weight):
        def product(part, start):
            return jnp.dot(acts_parts[part], columns(weight, start), preferred_element_type=f32)
        return product

    def backward(part, start):
        return lax.dot_general(
            cot_parts[part], rows(down_weight, start), (((1,), (1,)), ((), ())), preferred_element_type=f32
        )

    kinds = {"gate": forward(gate_weight), "up": forward(up_weight), "error": backward}
    for index in range(probes.shape[0]):
        kinds["tangent", index] = forward(probes[index])
    tangent_names = [("tangent", index) for index in range(probes.shape[0])]
    summed = {}

    def reduce(units, part):
        count = acts_parts[part].shape[0]

        def pieces(array):
            return [array[index * count : (index + 1) * count] for index in range(len(units))]

        going = [kinds[name](part, others(bases[which])).astype(NEAR) for name, which in units]
        came = pieces(swap(jnp.concatenate(going, axis=0), "col", 1))
        both = [
            kinds[name](part, own(bases[which])) + other.astype(f32) for (name, which), other in zip(units, came)
        ]
        crossing_parts = [pick(value, 1 - far).astype(FAR) for value in both]
        crossed = pieces(crossing(jnp.concatenate(crossing_parts, axis=0)))
        for (name, which), value, other in zip(units, both, crossed):
            summed[name, which, part] = (pick(value, far), other)

    def total(name, which):
        parts = [summed[name, which, part] for part in range(2)]
        return jnp.concatenate([kept + crossed.astype(f32) for kept, crossed in parts], axis=0)

    def begin(values):
        value = jnp.concatenate(values, axis=0)
        return value, crossing(value)

    def finish(begun, after):
        value, crossed = begun
        crossed, *_ = lax.optimization_barrier((crossed, *after))
        both = jnp.zeros((value.shape[0], half), value.dtype)
        both = lax.dynamic_update_slice_in_dim(both, value, far * quarter, axis=1)
        both = lax.dynamic_update_slice_in_dim(both, crossed, (1 - far) * quarter, axis=1)
        other = swap(both, "col", 1)
        return [
            tuple(side[index * tokens : (index + 1) * tokens] for side in (both, other))
            for index in range(value.shape[0] // tokens)
        ]

    reduce([(name, which) for which in range(2) for name in ("gate", "up")], 0)
    acts_parts[0], cot_parts[0], _ = lax.optimization_barrier((acts_parts[0], cot_parts[0], sent[-1]))
    reduce([(name, which) for which in range(2) for name in tangent_names + ["error"]], 0)
    for which in range(2):
        reduce([("gate", which), ("up", which)], 1)
    reduce([(name, 0) for name in tangent_names], 1)
    reduce([("error", 0)], 1)
    gates = [total("gate", which) for which in range(2)]
    ups = [total("up", which) for which in range(2)]
    sigmas = [jax.nn.sigmoid(gate) for gate in gates]
    units = [(gate * sigma * up).astype(bf16) for gate, sigma, up in zip(gates, sigmas, ups)]
    begun_hidden = begin(units)

    scale = 1.0 / (probes.shape[0] * lax.axis_size("dp") * tokens)

    def weighted(which):
        gate, sigma, up = gates[which], sigmas[which], ups[which]
        bending = total("error", which) * up * sigma * (1.0 - sigma) * (2.0 + gate * (1.0 - 2.0 * sigma))
        return begin([(bending * total(name, which)).astype(bf16) for name in tangent_names])

    def estimate(pieces, which, side):
        start = (own, others)[side](bases[which])
        result = 0.0
        for probe, piece in zip(probes, pieces):
            curvature = lax.dot_general(features, piece[side], (((0,), (0,)), ((), ())), preferred_element_type=f32)
            result = result + columns(probe, start).astype(f32) * curvature
        return result * scale

    begun_first = weighted(0)
    reduce([(name, 1) for name in tangent_names], 1)
    hidden = [side for sides in finish(begun_hidden, sent[-1:]) for side in sides]
    order = [place(base) for base in bases for place in (own, others)]
    down = jnp.concatenate([rows(down_weight, start) for start in order], axis=0)
    partial = jnp.dot(jnp.concatenate(hidden, axis=1), down, preferred_element_type=f32)
    partial = turned(partial, tokens - row * mine)
    outputs = lax.psum_scatter(partial, "row", scatter_dimension=0, tiled=True).astype(bf16)[None]
    reduce([("error", 1)], 1)
    pieces = finish(begun_first, sent[-1:])
    begun_second = weighted(1)
    early = [estimate(pieces, 0, side).astype(bf16) for side in range(2)]
    came = [swap(value, "dp", 1).astype(f32) for value in early]
    pieces = finish(begun_second, early)
    first, second = [estimate(pieces, 1, side) + came[side] for side in range(2)]
    diagonal = jnp.where(
        near == 0,
        jnp.concatenate([first, second], axis=1),
        jnp.concatenate([second, first], axis=1),
    )
    return outputs, diagonal


def solution(mesh):
    in_specs = (
        P("dp", "row", "col"),
        P("dp", "row", "col"),
        P("col", "row"),
        P("col", "row"),
        P("row", "col"),
        P(None, "col", "row"),
    )
    out_specs = (P("dp", "row", "col"), P("col", ("row", "dp")))
    return jax.shard_map(local, mesh=mesh, in_specs=in_specs, out_specs=out_specs, check_vma=False)
```
